32 devices in a mesh: vid: 16 (over z, y, core), aud: 2 (over x).
Axes of the slice: x: 2, y: 2, z: 4, core: 2. Of those that a mesh axis runs over, the one named last changes fastest.
Arguments:
- q_video: bfloat16 [4096, 1536], P('vid', 'aud'), may hold values from -240 to 240
- video_key_rows: bfloat16 [4096, 1536], P('vid', 'aud'), may hold values from -6 to 6
- video_value_rows: bfloat16 [4096, 1536], P('vid', 'aud'), may hold values from -6 to 6
- g_video: bfloat16 [4096, 1536], P('vid', 'aud'), may hold values from -6 to 6
- q_audio: bfloat16 [1024, 1536], P(('vid', 'aud')), may hold values from -240 to 240
- k_audio: bfloat16 [1024, 1536], P(('vid', 'aud')), may hold values from -6 to 6
- v_audio: bfloat16 [1024, 1536], P(('vid', 'aud')), may hold values from -6 to 6
- g_audio: bfloat16 [1024, 1536], P(('vid', 'aud')), may hold values from -6 to 6
- window: int32 [64, 2], replicated, may hold values from 0 to 15, as said below
- audio_len: int32 [16], replicated, may hold values from 1 to 64
Outputs:
- out_video: bfloat16 [4096, 1536], P('vid', 'aud')
- out_audio: bfloat16 [1024, 1536], P(('vid', 'aud'))
- dq_video: bfloat16 [4096, 1536], P('vid', 'aud')
- dk_video: bfloat16 [4096, 1536], P('vid', 'aud')
- dv_video: bfloat16 [4096, 1536], P('vid', 'aud')
- dq_audio: bfloat16 [1024, 1536], P(('vid', 'aud'))
- dk_audio: bfloat16 [1024, 1536], P(('vid', 'aud'))
- dv_audio: bfloat16 [1024, 1536], P(('vid', 'aud'))
The draws below stay inside these ranges and needn't reach their ends.
Inputs may be any that keep to these rules, and one draw needn't show every extreme that they name: window[i] = (start, count) with 1 <= count <= 3 (3 is reached in every draw), start <= i // 4 < start + count, and start + count <= 16.
All inputs are finite; a program needn't handle non-finite values.
Results may differ from the reference program's by a relative error of at most 0.0095.
Values may be sent and summed in bfloat16 or wider, within the bound.
A program may use at most 64 MiB of HBM per device.

```python
import jax
import jax.numpy as jnp
from jax import lax

HD = 64
D = 1536
BLK = 64
WMAX = 3
ABLK = 16
VBLK = 64
ATOK = 1024
VTOK = 4096


def normal_block(key, tag, height, width):
    drawn = jax.random.normal(jax.random.fold_in(key, tag), (height, width), jnp.float32)
    return jnp.clip(drawn, -6.0, 6.0)


def draw_video_key_rows(key, part):
    return normal_block(key, 11, VTOK, D).astype(jnp.bfloat16)


def draw_k_audio(key, part):
    return normal_block(key, 12, ATOK, D).astype(jnp.bfloat16)


def draw_q_video(key, part):
    drawn = normal_block(key, 13, VTOK, D)
    return drawn.astype(jnp.bfloat16)


def draw_q_audio(key, part):
    drawn = normal_block(key, 15, ATOK, D)
    return drawn.astype(jnp.bfloat16)


def draw_window(key, part):
    block_ids = jnp.arange(VBLK)
    number = jax.random.randint(jax.random.fold_in(key, 21), (VBLK,), 1, WMAX + 1)
    number = jnp.where(block_ids % 16 == 3, WMAX, number)
    window_shift = jax.random.randint(jax.random.fold_in(key, 22), (VBLK,), 0, WMAX) % number
    first = jnp.clip(block_ids // 4 - window_shift, 0, ABLK - number)
    return jnp.stack([first, number], axis=1).astype(jnp.int32)


def draw_audio_len(key, part):
    lengths = jax.random.randint(jax.random.fold_in(key, 23), (ABLK,), 1, BLK + 1)
    lengths = jnp.where(jnp.arange(ABLK) % 8 == 0, BLK, lengths)
    return lengths.astype(jnp.int32)


def level_of(own_key, shape, cuts, smallest, largest):
    def one(position, shards_of):
        heights = jax.random.uniform(jax.random.fold_in(jax.random.fold_in(own_key, 6), position), (shards_of,), jnp.float32, smallest / len(cuts), largest / len(cuts))
        return jnp.repeat(jnp.exp(heights), shape[position] // shards_of).reshape((-1,) + (1,) * (len(shape) - position - 1))

    loudness = one(*cuts[0])
    for cut in cuts[1:]:
        loudness = loudness * one(*cut)
    return loudness


def normal_values(key, dims, scale, reach, split=(), held_as=jnp.bfloat16):
    values = scale * jax.random.normal(key, dims, jnp.float32)
    if split:
        values = values * level_of(key, dims, split, -0.22, 0.18)
    return jnp.clip(values, -reach, reach).astype(held_as)


def setup_inputs(seed: int = 0) -> dict:
    splits = jax.random.split(jax.random.key(seed), 11)
    return {
        "q_video": draw_q_video(jax.random.fold_in(splits[10], 71), 0),
        "video_key_rows": draw_video_key_rows(jax.random.fold_in(splits[10], 71), 0),
        "video_value_rows": normal_values(splits[2], (VTOK, D), 1.0, 6.0, ((0, 16), (1, 2))),
        "g_video": normal_values(splits[3], (VTOK, D), 1.0, 6.0, ((0, 16), (1, 2))),
        "q_audio": draw_q_audio(jax.random.fold_in(splits[10], 71), 0),
        "k_audio": draw_k_audio(jax.random.fold_in(splits[10], 71), 0),
        "v_audio": normal_values(splits[6], (ATOK, D), 1.0, 6.0, ((0, 32),)),
        "g_audio": normal_values(splits[7], (ATOK, D), 1.0, 6.0, ((0, 32),)),
        "window": draw_window(jax.random.fold_in(splits[10], 71), 0),
        "audio_len": draw_audio_len(jax.random.fold_in(splits[10], 71), 0),
    }


NEG_FILL = -1.0e30


def split_heads(matrix):
    return matrix.astype(jnp.float32).reshape(matrix.shape[0], matrix.shape[1] // HD, HD)


def flatten_heads(tensor):
    return tensor.reshape(tensor.shape[0], -1)


def pair_block(queries, key_rows, value_rows, cotangent, allowed, query_valid):
    scale = HD ** -0.5
    q_heads = split_heads(queries)
    k_heads = split_heads(key_rows)
    v_heads = split_heads(value_rows)
    g_heads = split_heads(cotangent) * query_valid[:, None, None]
    scores = jnp.einsum("rhd,khd->hrk", q_heads, k_heads) * scale
    scores = jnp.where(allowed[None], scores, NEG_FILL)
    row_max = jnp.max(scores, axis=2, keepdims=True)
    row_sum = jnp.sum(jnp.where(allowed[None], jnp.exp(scores - row_max), 0.0), axis=2, keepdims=True)
    attention_probs = jnp.where(allowed[None], jnp.exp(scores - (row_max + jnp.log(row_sum))), 0.0)
    weights_b = lax.optimization_barrier(attention_probs.astype(jnp.bfloat16)).astype(jnp.float32)
    mixed = jnp.einsum("hrk,khd->rhd", weights_b, v_heads) * query_valid[:, None, None]
    out_rows = flatten_heads(mixed).astype(jnp.bfloat16)
    deltas = jnp.sum(g_heads * split_heads(out_rows), axis=2)
    grad_p = jnp.einsum("rhd,khd->hrk", g_heads, v_heads)
    grad_s = (attention_probs * (grad_p - deltas.T[:, :, None])).astype(jnp.bfloat16)
    grad_s = lax.optimization_barrier(grad_s).astype(jnp.float32)
    grad_q = jnp.einsum("hrk,khd->rhd", grad_s, k_heads) * scale
    grad_k = jnp.einsum("hrk,rhd->khd", grad_s, q_heads) * scale
    grad_v = jnp.einsum("hrk,rhd->khd", weights_b, g_heads)
    return out_rows, flatten_heads(grad_q), flatten_heads(grad_k), flatten_heads(grad_v)


def add_rows(accum, piece, start):
    current = lax.dynamic_slice_in_dim(accum, start, piece.shape[0], 0)
    return lax.dynamic_update_slice_in_dim(accum, current + piece, start, 0)


def reference(q_video, video_key_rows, video_value_rows, g_video, q_audio, k_audio, v_audio, g_audio, window, audio_len):
    audio_count = audio_len.shape[0]
    video_count = window.shape[0]
    width = q_video.shape[1]
    span = 2 * WMAX - 1
    group = 4 * BLK
    pad_audio = (WMAX - 1) * BLK
    pad_video = (WMAX - 1) * group
    starts = window[:, 0]
    counts = window[:, 1]
    k_audio_pad = jnp.pad(k_audio, ((pad_audio, pad_audio), (0, 0)))
    v_audio_pad = jnp.pad(v_audio, ((pad_audio, pad_audio), (0, 0)))
    k_video_pad = jnp.pad(video_key_rows, ((pad_video, pad_video), (0, 0)))
    v_video_pad = jnp.pad(video_value_rows, ((pad_video, pad_video), (0, 0)))
    token_pos = jnp.arange(span * BLK) % BLK

    def video_step(carry, index):
        grad_k_acc, grad_v_acc = carry
        queries = lax.dynamic_slice_in_dim(q_video, index * group, group, 0)
        cotangent = lax.dynamic_slice_in_dim(g_video, index * group, group, 0)
        key_rows = lax.dynamic_slice_in_dim(k_audio_pad, index * BLK, span * BLK, 0)
        value_rows = lax.dynamic_slice_in_dim(v_audio_pad, index * BLK, span * BLK, 0)
        first = lax.dynamic_slice_in_dim(starts, index * 4, 4, 0)
        number = lax.dynamic_slice_in_dim(counts, index * 4, 4, 0)
        audio_ids = index - (WMAX - 1) + jnp.arange(span)
        block_ok = (audio_ids[None] >= first[:, None]) & (audio_ids[None] < first[:, None] + number[:, None])
        lengths = jnp.take(audio_len, jnp.clip(audio_ids, 0, audio_count - 1))
        key_ok = token_pos < jnp.repeat(lengths, BLK)
        allowed = jnp.repeat(jnp.repeat(block_ok, BLK, 0), BLK, 1) & key_ok[None]
        out_rows, grad_q, grad_k, grad_v = pair_block(queries, key_rows, value_rows, cotangent, allowed, jnp.ones((group,), jnp.float32))
        grad_k_acc = add_rows(grad_k_acc, grad_k, index * BLK)
        grad_v_acc = add_rows(grad_v_acc, grad_v, index * BLK)
        return (grad_k_acc, grad_v_acc), (out_rows, grad_q.astype(jnp.bfloat16))

    def audio_step(carry, index):
        grad_k_acc, grad_v_acc = carry
        queries = lax.dynamic_slice_in_dim(q_audio, index * BLK, BLK, 0)
        cotangent = lax.dynamic_slice_in_dim(g_audio, index * BLK, BLK, 0)
        key_rows = lax.dynamic_slice_in_dim(k_video_pad, index * group, span * group, 0)
        value_rows = lax.dynamic_slice_in_dim(v_video_pad, index * group, span * group, 0)
        video_ids = 4 * (index - (WMAX - 1)) + jnp.arange(4 * span)
        inside = (video_ids >= 0) & (video_ids < video_count)
        clipped = jnp.clip(video_ids, 0, video_count - 1)
        first = jnp.take(starts, clipped)
        number = jnp.take(counts, clipped)
        block_ok = inside & (index >= first) & (index < first + number)
        allowed = jnp.broadcast_to(jnp.repeat(block_ok, BLK)[None], (BLK, span * group))
        query_valid = (jnp.arange(BLK) < audio_len[index]).astype(jnp.float32)
        out_rows, grad_q, grad_k, grad_v = pair_block(queries, key_rows, value_rows, cotangent, allowed, query_valid)
        grad_k_acc = add_rows(grad_k_acc, grad_k, index * group)
        grad_v_acc = add_rows(grad_v_acc, grad_v, index * group)
        return (grad_k_acc, grad_v_acc), (out_rows, grad_q.astype(jnp.bfloat16))

    audio_zero = jnp.zeros((audio_count * BLK + 2 * pad_audio, width), jnp.float32)
    (dk_a, dv_a), (out_v, dq_v) = lax.scan(video_step, (audio_zero, audio_zero), jnp.arange(audio_count, dtype=jnp.int32))
    video_zero = jnp.zeros((video_count * BLK + 2 * pad_video, width), jnp.float32)
    (dk_v, dv_v), (out_a, dq_a) = lax.scan(audio_step, (video_zero, video_zero), jnp.arange(audio_count, dtype=jnp.int32))
    audio_tokens = audio_count * BLK
    video_tokens = video_count * BLK
    out_video = out_v.reshape(video_tokens, width)
    dq_video = dq_v.reshape(video_tokens, width)
    out_audio = out_a.reshape(audio_tokens, width)
    dq_audio = dq_a.reshape(audio_tokens, width)
    dk_audio = dk_a[pad_audio:pad_audio + audio_tokens].astype(jnp.bfloat16)
    dv_audio = dv_a[pad_audio:pad_audio + audio_tokens].astype(jnp.bfloat16)
    dk_video = dk_v[pad_video:pad_video + video_tokens].astype(jnp.bfloat16)
    dv_video = dv_v[pad_video:pad_video + video_tokens].astype(jnp.bfloat16)
    return (out_video, out_audio, dq_video, dk_video, dv_video, dq_audio, dk_audio, dv_audio)
```

```python
import functools

import jax
import jax.numpy as jnp
from jax import lax
from jax.experimental import pallas as pl
from jax.experimental.pallas import tpu as pltpu
from jax.sharding import PartitionSpec as P

HD = 64
BLK = 64
WMAX = 3
NEG = -1e30
FLOOR = -1e29
REACH = WMAX - 1
SLOTS = 2 * REACH + 1
OWN = REACH
PAIR = 2 * HD

F32 = jnp.float32
BF16 = jnp.bfloat16


def dot_nt(a, b):
    return lax.dot_general(a, b, (((1,), (1,)), ((), ())), preferred_element_type=F32)


def dot_nn(a, b):
    return lax.dot_general(a, b, (((1,), (0,)), ((), ())), preferred_element_type=F32)


def dot_tn(a, b):
    return lax.dot_general(a, b, (((0,), (0,)), ((), ())), preferred_element_type=F32)


def kernel(
    n,
    win,
    alen,
    qv,
    kv,
    vv,
    gv,
    qa,
    ka,
    va,
    ga,
    out_v,
    out_a,
    dq_v,
    dk_v,
    dv_v,
    dq_a,
    dk_a,
    dv_a,
    near,
    e_buf,
    dp_buf,
    bias_va,
    bias_av,
    vmask,
    stats,
    stats_in,
    res,
    part,
    sendb,
    mate_in,
    far_in,
    fin,
    x_send,
    x_recv,
    far_send,
    far_recv,
    mate_send,
    mate_recv,
    relay_send,
    relay_recv,
    st_send,
    st_recv,
    rs_send,
    rs_recv,
    rm_send,
    rm_recv,
    rf_send,
    rf_recv,
    xo_send,
    xo_recv,
):
    d = lax.axis_index("vid")
    a = lax.axis_index("aud")
    odd = lax.rem(d, 2)
    mate = d + 1 - 2 * odd
    peer = 1 - a
    half = qa.shape[0]
    width = qv.shape[1]
    vrows = qv.shape[0]
    arows = 2 * half
    vblocks = vrows // BLK
    heads = width // HD
    pairs = width // PAIR
    has = {o: (d + o >= 0) & (d + o < n) for o in (-2, -1, 1, 2)}

    def at(vid):
        return {"vid": vid, "aud": a}

    def remote(src, dst, s, r, dev):
        return pltpu.make_async_remote_copy(
            src_ref=src,
            dst_ref=dst,
            send_sem=s,
            recv_sem=r,
            device_id=dev,
            device_id_type=pl.DeviceIdType.MESH,
        )

    def rows(slot, t, size):
        return pl.ds(pl.multiple_of(slot * arows + t * half, half), size)

    barrier = pltpu.get_barrier_semaphore()
    pl.semaphore_signal(
        barrier, inc=1, device_id={"vid": d, "aud": peer}, device_id_type=pl.DeviceIdType.MESH
    )
    for o in has:

        @pl.when(has[o])
        def _(o=o):
            pl.semaphore_signal(
                barrier, inc=1, device_id=at(d + o), device_id_type=pl.DeviceIdType.MESH
            )

    ins = (qa, ga, ka, va)
    own_cols = pl.ds(pl.multiple_of(a * width, width), width)
    peer_cols = pl.ds(pl.multiple_of(peer * width, width), width)
    for t in range(4):
        near[t, rows(OWN, a, half), :] = ins[t][:, own_cols]

    pl.semaphore_wait(barrier, 1 + sum(jnp.where(has[o], 1, 0) for o in has))

    x_copy = [
        remote(
            ins[t].at[:, peer_cols],
            near.at[t, rows(OWN, a, half)],
            x_send.at[t],
            x_recv.at[t],
            {"vid": d, "aud": peer},
        )
        for t in range(4)
    ]

    def x_arrived(t):
        return remote(
            ins[t].at[:, own_cols],
            near.at[t, rows(OWN, peer, half)],
            x_send.at[t],
            x_recv.at[t],
            {"vid": d, "aud": peer},
        )

    def piece(group, slot, which):
        return near.at[pl.ds(2 * group, 2), rows(slot, a if which == 0 else peer, half)]

    def far_copy(group, which, side):
        o = (-2, 2)[side]
        return remote(
            piece(group, OWN, which),
            piece(group, OWN - o, which),
            far_send.at[group, which, side],
            far_recv.at[group, which, 1 - side],
            at(d + o),
        )

    def far_arrived(group, which, side):
        o = (-2, 2)[side]
        return remote(
            piece(group, OWN, which),
            piece(group, OWN + o, which),
            far_send.at[group, which, side],
            far_recv.at[group, which, side],
            at(d + o),
        )

    def mate_copy(group, which, slot):
        return remote(
            piece(group, OWN, which),
            piece(group, slot, which),
            mate_send.at[group, which],
            mate_recv.at[group, which],
            at(mate),
        )

    def relay_copy(group, which, src_slot, slot):
        return remote(
            piece(group, src_slot, which),
            piece(group, slot, which),
            relay_send.at[group, which],
            relay_recv.at[group, which],
            at(mate),
        )

    low_slot = 1 + 2 * odd
    high_slot = 3 - 2 * odd
    relay_from = 4 - 4 * odd
    relays_out = ((odd == 0) & has[2]) | ((odd == 1) & has[-2])
    relays_in = ((odd == 0) & has[-1]) | ((odd == 1) & has[1])

    def send_own(group, which):
        for side in range(2):

            @pl.when(has[(-2, 2)[side]])
            def _(side=side):
                far_copy(group, which, side).start()

        mate_copy(group, which, low_slot).start()

    def take_and_relay(group, which):
        for side in range(2):

            @pl.when(has[(-2, 2)[side]])
            def _(side=side):
                far_arrived(group, which, side).wait_recv()

        @pl.when(relays_out)
        def _():
            relay_copy(group, which, relay_from, low_slot + 2 * (1 - 2 * odd)).start()

    def finish_group(group):
        for which in range(2):
            mate_copy(group, which, high_slot).wait_recv()

            @pl.when(relays_in)
            def _(which=which):
                relay_copy(group, which, relay_from, low_slot).wait_recv()

    x_copy[0].start()
    x_copy[1].start()
    send_own(0, 0)
    x_copy[2].start()
    x_copy[3].start()

    for slot in range(SLOTS):
        o = slot - OWN
        if o != 0:

            @pl.when(jnp.logical_not(has[o]))
            def _(slot=slot):
                span = pl.ds(slot * arows, arows)
                near[:, span, :] = jnp.zeros((4, arows, width), BF16)
                stats_in[span, :] = jnp.full((arows, 128), NEG, F32)
                res[span, :] = jnp.zeros((arows, 128), F32)

    for side in range(2):

        @pl.when(jnp.logical_not(has[(-2, 2)[side]]))
        def _(side=side):
            far_in[:, side] = jnp.zeros((2, 2, arows, width), BF16)

    vb = lax.broadcasted_iota(jnp.int32, (arows, vrows), 1) // BLK
    tok = lax.broadcasted_iota(jnp.int32, (arows, vrows), 0)
    tok_l = lax.broadcasted_iota(jnp.int32, (arows, PAIR), 0)
    lens = []
    for slot in range(SLOTS):
        ablk = d + (slot - OWN)
        length = alen[lax.rem(ablk + n, n)]
        lens.append(length)
        bias = jnp.full((arows, vrows), NEG, F32)
        for b in range(vblocks):
            first = win[d * vblocks + b, 0]
            number = win[d * vblocks + b, 1]
            ok = (ablk >= first) & (ablk < first + number)
            bias = jnp.where(vb == b, jnp.where(ok, 0.0, NEG), bias)
        span = pl.ds(slot * arows, arows)
        bias_av[span, :] = bias
        bias_va[span, :] = jnp.where(tok < length, bias, NEG)
        vmask[span, :] = jnp.where(tok_l < length, 1.0, 0.0).astype(BF16)

    lane_w = lax.broadcasted_iota(jnp.int32, (1, PAIR), 1)
    half_mask = [
        jnp.where((lane_w >= HD * h) & (lane_w < HD * (h + 1)), 1.0, 0.0).astype(BF16)
        for h in range(2)
    ]
    lane_s = lax.broadcasted_iota(jnp.int32, (SLOTS * arows, 128), 1)
    stats[...] = jnp.zeros_like(stats)

    def both(low, high):
        lane = lax.broadcasted_iota(jnp.int32, low.shape, 1)
        return jnp.where(lane < HD, low, high)

    x_arrived(0).wait_recv()
    x_arrived(1).wait_recv()
    send_own(0, 1)
    send_own(1, 0)
    take_and_relay(0, 0)
    x_arrived(2).wait_recv()
    x_arrived(3).wait_recv()
    send_own(1, 1)
    take_and_relay(0, 1)
    finish_group(0)

    scale = HD**-0.5

    def cols(i):
        return pl.ds(pl.multiple_of(i * PAIR, PAIR), PAIR)

    def av_scores(i, carry):
        c = cols(i)
        q = near[0, :, c] * jnp.asarray(scale, BF16)
        g = near[1, :, c] * vmask[...]
        k = kv[:, c]
        v = vv[:, c]
        for h in range(2):
            s = dot_nt(q * half_mask[h], k) + bias_av[...]
            dp = dot_nt(g * half_mask[h], v)
            m = jnp.maximum(jnp.max(s, axis=1, keepdims=True), FLOOR)
            e = jnp.exp(s - m)
            total = jnp.sum(e, axis=1, keepdims=True)
            mixed = jnp.sum(e * dp, axis=1, keepdims=True)
            e_buf[2 * i + h] = e
            dp_buf[2 * i + h] = dp
            head = 2 * i + h
            old = stats[...]
            old = jnp.where(lane_s == head, m, old)
            old = jnp.where(lane_s == head + heads, total, old)
            stats[...] = jnp.where(lane_s == head + 2 * heads, mixed, old)
        return carry

    lax.fori_loop(0, pairs, av_scores, 0)

    def stats_copy(o):
        src = pl.ds((OWN + o) * arows, arows)
        dst = pl.ds((OWN - o) * arows, arows)
        return remote(
            stats.at[src], stats_in.at[dst], st_send.at[OWN + o], st_recv.at[OWN - o], at(d + o)
        )

    def stats_arrived(o):
        span = pl.ds((OWN + o) * arows, arows)
        return remote(
            stats.at[span], stats_in.at[span], st_send.at[OWN + o], st_recv.at[OWN + o], at(d + o)
        )

    def res_copy(o):
        return remote(
            res.at[pl.ds(OWN * arows, arows)],
            res.at[pl.ds((OWN - o) * arows, arows)],
            rs_send.at[OWN + o],
            rs_recv.at[OWN - o],
            at(d + o),
        )

    def res_arrived(o):
        return remote(
            res.at[pl.ds(OWN * arows, arows)],
            res.at[pl.ds((OWN + o) * arows, arows)],
            rs_send.at[OWN + o],
            rs_recv.at[OWN + o],
            at(d + o),
        )

    def each(make, action):
        for o in has:

            @pl.when(has[o])
            def _(o=o):
                action(make(o))

    each(stats_copy, lambda c: c.start())
    own_span = pl.ds(OWN * arows, arows)
    stats_in[own_span, :] = stats[own_span, :]

    take_and_relay(1, 0)
    take_and_relay(1, 1)
    finish_group(1)

    def store_part(kind, member, c, value):
        part[kind, member, :, c] = value
        sendb[kind, member, :, c] = value.astype(BF16)

    def va_all(i, carry):
        c = cols(i)
        k = near[2, :, c]
        v = near[3, :, c]
        q = qv[:, c] * jnp.asarray(scale, BF16)
        g = gv[:, c]
        o, dq, dk, dv = [], [], [], []
        for h in range(2):
            s = dot_nt(k * half_mask[h], q) + bias_va[...]
            dp = dot_nt(v * half_mask[h], g)
            m = jnp.max(s, axis=0, keepdims=True)
            e = jnp.exp(s - m)
            p = e * (1.0 / jnp.sum(e, axis=0, keepdims=True))
            delta = jnp.sum(p * dp, axis=0, keepdims=True)
            pb = p.astype(BF16)
            ds = (p * (dp - delta)).astype(BF16)
            o.append(dot_tn(pb, v))
            dq.append(dot_tn(ds, k))
            dk.append(dot_nn(ds, q))
            dv.append(dot_nn(pb, g))
        out_v[:, c] = both(*o).astype(BF16)
        dq_v[:, c] = (both(*dq) * scale).astype(BF16)
        store_part(0, 0, c, both(*dk))
        store_part(0, 1, c, both(*dv))
        return carry

    lax.fori_loop(0, pairs // 2, va_all, 0)

    each(stats_arrived, lambda c: c.wait_recv())
    parts = [stats_in[pl.ds(slot * arows, arows), :] for slot in range(SLOTS)]
    top = functools.reduce(jnp.maximum, parts)
    total = jnp.zeros_like(top)
    mixed = jnp.zeros_like(top)
    for x in parts:
        weight = jnp.exp(x - top)
        total = total + weight * pltpu.roll(x, 128 - heads, 1)
        mixed = mixed + weight * pltpu.roll(x, 128 - 2 * heads, 1)
    lane_o = lax.broadcasted_iota(jnp.int32, top.shape, 1)
    res[own_span, :] = jnp.where(
        lane_o < heads, top + jnp.log(total), pltpu.roll(mixed / total, heads, 1)
    )
    each(res_copy, lambda c: c.start())

    lax.fori_loop(pairs // 2, pairs, va_all, 0)

    def rm_copy(kind, to_owner, src_slot):
        span = pl.ds(pl.multiple_of(src_slot * arows, arows), arows)
        return remote(
            sendb.at[kind, :, span],
            mate_in.at[kind, to_owner],
            rm_send.at[kind, to_owner],
            rm_recv.at[kind, to_owner],
            at(mate),
        )

    def rf_copy(kind, side):
        slot = (0, 4)[side]
        return remote(
            sendb.at[kind, :, pl.ds(slot * arows, arows)],
            far_in.at[kind, 1 - side],
            rf_send.at[kind, side],
            rf_recv.at[kind, 1 - side],
            at(d + (-2, 2)[side]),
        )

    def rf_arrived(kind, side):
        return remote(
            sendb.at[kind, :, pl.ds(0, arows)],
            far_in.at[kind, side],
            rf_send.at[kind, side],
            rf_recv.at[kind, side],
            at(d + (-2, 2)[side]),
        )

    def return_first(kind):
        @pl.when(relays_in)
        def _():
            rm_copy(kind, 0, low_slot).start()

        @pl.when((odd == 0) & has[-2])
        def _():
            rf_copy(kind, 0).start()

        @pl.when((odd == 1) & has[2])
        def _():
            rf_copy(kind, 1).start()

        rm_copy(kind, 1, high_slot).start()

    def return_second(kind):
        for side, parity in ((1, 0), (0, 1)):

            @pl.when((odd == parity) & has[(-2, 2)[side]])
            def _(side=side):
                rm_copy(kind, 0, low_slot).wait_recv()
                span = pl.ds((0, 4)[side] * arows, arows)
                for member in range(2):
                    sendb[kind, member, span, :] = (
                        part[kind, member, span, :] + mate_in[kind, 0, member].astype(F32)
                    ).astype(BF16)
                rf_copy(kind, side).start()

    finals = ((dk_a, dv_a), (out_a, dq_a))

    def xo_copy(kind, member):
        return remote(
            fin.at[kind, member, pl.ds(pl.multiple_of(peer * half, half), half)],
            finals[kind][member].at[:, own_cols],
            xo_send.at[kind, member],
            xo_recv.at[kind, member],
            {"vid": d, "aud": peer},
        )

    def xo_arrived(kind, member):
        return remote(
            fin.at[kind, member, pl.ds(pl.multiple_of(peer * half, half), half)],
            finals[kind][member].at[:, peer_cols],
            xo_send.at[kind, member],
            xo_recv.at[kind, member],
            {"vid": d, "aud": peer},
        )

    def return_last(kind):
        rm_copy(kind, 1, high_slot).wait_recv()
        for side in range(2):

            @pl.when(has[(-2, 2)[side]])
            def _(side=side):
                rf_arrived(kind, side).wait_recv()

        for member in range(2):
            value = (
                part[kind, member, own_span, :]
                + mate_in[kind, 1, member].astype(F32)
                + far_in[kind, 0, member].astype(F32)
                + far_in[kind, 1, member].astype(F32)
            )
            if kind == 1 and member == 0:
                token = lax.broadcasted_iota(jnp.int32, value.shape, 0)
                value = jnp.where(token < lens[OWN], value, 0.0)
            fin[kind, member] = value.astype(BF16)
            xo_copy(kind, member).start()
            finals[kind][member][:, own_cols] = fin[
                kind, member, pl.ds(pl.multiple_of(a * half, half), half), :
            ]

    return_first(0)
    each(res_arrived, lambda c: c.wait_recv())

    def av_all(i, carry):
        c = cols(i)
        q = near[0, :, c] * jnp.asarray(scale, BF16)
        g = near[1, :, c] * vmask[...]
        k = kv[:, c]
        v = vv[:, c]
        o, dq, dk, dv = [], [], [], []
        lane = lax.broadcasted_iota(jnp.int32, (SLOTS * arows, 128), 1)
        for h in range(2):
            head = 2 * i + h
            gap = jnp.sum(jnp.where(lane == head, stats[...] - res[...], 0.0), 1, keepdims=True)
            delta = jnp.sum(jnp.where(lane == head + heads, res[...], 0.0), 1, keepdims=True)
            p = e_buf[head] * jnp.exp(gap)
            pb = p.astype(BF16)
            ds = (p * (dp_buf[head] - delta)).astype(BF16)
            o.append(dot_nn(pb, v))
            dq.append(dot_nn(ds, k))
            dk.append(dot_tn(ds, q))
            dv.append(dot_tn(pb, g))
        store_part(1, 0, c, both(*o))
        store_part(1, 1, c, both(*dq) * scale)
        dk_v[:, c] = both(*dk).astype(BF16)
        dv_v[:, c] = both(*dv).astype(BF16)
        return carry

    lax.fori_loop(0, pairs // 2, av_all, 0)
    return_second(0)
    lax.fori_loop(pairs // 2, pairs, av_all, 0)
    return_first(1)
    return_second(1)
    return_last(0)
    return_last(1)
    for kind in range(2):
        for member in range(2):
            xo_arrived(kind, member).wait_recv()

    for t in range(4):
        x_copy[t].wait_send()
    for group in range(2):
        for which in range(2):
            for side in range(2):

                @pl.when(has[(-2, 2)[side]])
                def _(group=group, which=which, side=side):
                    far_copy(group, which, side).wait_send()

            mate_copy(group, which, low_slot).wait_send()

            @pl.when(relays_out)
            def _(group=group, which=which):
                relay_copy(group, which, relay_from, high_slot).wait_send()

    each(stats_copy, lambda c: c.wait_send())
    each(res_copy, lambda c: c.wait_send())
    for kind in range(2):

        @pl.when(relays_in)
        def _(kind=kind):
            rm_copy(kind, 0, low_slot).wait_send()

        rm_copy(kind, 1, high_slot).wait_send()
        for side in range(2):

            @pl.when(has[(-2, 2)[side]])
            def _(kind=kind, side=side):
                rf_copy(kind, side).wait_send()

        for member in range(2):
            xo_copy(kind, member).wait_send()


def body(n, q_video, k_video, v_video, g_video, q_audio, k_audio, v_audio, g_audio, window, alen):
    vrows, width = q_video.shape
    half, full = q_audio.shape
    arows = 2 * half
    heads = width // HD
    near_rows = SLOTS * arows
    assert arows == BLK and n % 2 == 0 and 3 * heads <= 128 and width % (2 * PAIR) == 0
    video = jax.ShapeDtypeStruct((vrows, width), BF16)
    audio = jax.ShapeDtypeStruct((half, full), BF16)
    dma = pltpu.SemaphoreType.DMA
    vmem = pl.BlockSpec(memory_space=pltpu.VMEM)
    smem = pl.BlockSpec(memory_space=pltpu.SMEM)
    sems = [(4,), (2, 2, 2), (2, 2), (2, 2), (SLOTS,), (SLOTS,), (2, 2), (2, 2), (2, 2)]
    return pl.pallas_call(
        functools.partial(kernel, n),
        out_shape=(video, audio, video, video, video, audio, audio, audio),
        in_specs=[smem] * 2 + [vmem] * 8,
        out_specs=(vmem,) * 8,
        scratch_shapes=[
            pltpu.VMEM((4, near_rows, width), BF16),
            pltpu.VMEM((heads, near_rows, vrows), F32),
            pltpu.VMEM((heads, near_rows, vrows), F32),
            pltpu.VMEM((near_rows, vrows), F32),
            pltpu.VMEM((near_rows, vrows), F32),
            pltpu.VMEM((near_rows, PAIR), BF16),
            pltpu.VMEM((near_rows, 128), F32),
            pltpu.VMEM((near_rows, 128), F32),
            pltpu.VMEM((near_rows, 128), F32),
            pltpu.VMEM((2, 2, near_rows, width), F32),
            pltpu.VMEM((2, 2, near_rows, width), BF16),
            pltpu.VMEM((2, 2, 2, arows, width), BF16),
            pltpu.VMEM((2, 2, 2, arows, width), BF16),
            pltpu.VMEM((2, 2, arows, width), BF16),
        ]
        + [dma(shape) for shape in sems for _ in range(2)],
        compiler_params=pltpu.CompilerParams(
            collective_id=0, has_side_effects=True, vmem_limit_bytes=48 * 1024 * 1024
        ),
    )(window, alen, q_video, k_video, v_video, g_video, q_audio, k_audio, v_audio, g_audio)


def solution(mesh):
    tokens = P("vid", "aud")
    stretch = P(("vid", "aud"), None)
    return jax.shard_map(
        functools.partial(body, mesh.shape["vid"]),
        mesh=mesh,
        in_specs=(tokens,) * 4 + (stretch,) * 4 + (P(), P()),
        out_specs=(tokens, stretch, tokens, tokens, tokens, stretch, stretch, stretch),
        check_vma=False,
    )
```

```python
import functools

import jax
import jax.numpy as jnp
from jax import lax
from jax.experimental import pallas as pl
from jax.experimental.pallas import tpu as pltpu
from jax.sharding import PartitionSpec as P

HD = 64
BLK = 64
WMAX = 3
NEG = -1e30
FLOOR = -1e29
REACH = WMAX - 1
SLOTS = 2 * REACH + 1
OWN = REACH
PAIR = 2 * HD
VMEM = 62 * 1024 * 1024

F32 = jnp.float32
BF16 = jnp.bfloat16


def dot_nt(a, b):
    return lax.dot_general(a, b, (((1,), (1,)), ((), ())), preferred_element_type=F32)


def dot_nn(a, b):
    return lax.dot_general(a, b, (((1,), (0,)), ((), ())), preferred_element_type=F32)


def dot_tn(a, b):
    return lax.dot_general(a, b, (((0,), (0,)), ((), ())), preferred_element_type=F32)


def kernel(
    n,
    win,
    alen,
    qv_in,
    kv_in,
    vv_in,
    gv_in,
    qa,
    ka,
    va,
    ga,
    out_v_hbm,
    out_a,
    dq_v_hbm,
    dk_v_hbm,
    dv_v_hbm,
    dq_a,
    dk_a,
    dv_a,
    near,
    e_buf,
    dp_buf,
    bias_va,
    bias_av,
    vmask,
    stats,
    stats_in,
    res,
    part,
    sendb,
    mate_in,
    far_in,
    fin,
    qv,
    kv,
    vv,
    gv,
    out_v,
    dq_v,
    dk_v,
    dv_v,
    own_sem,
    video_sem,
    write_sem,
    fin_sem,
    x_send,
    x_recv,
    far_send,
    far_recv,
    mate_send,
    mate_recv,
    relay_send,
    relay_recv,
    st_send,
    st_recv,
    rs_send,
    rs_recv,
    rm_send,
    rm_recv,
    rf_send,
    rf_recv,
    xo_send,
    xo_recv,
):
    d = lax.axis_index("vid")
    a = lax.axis_index("aud")
    odd = lax.rem(d, 2)
    mate = d + 1 - 2 * odd
    peer = 1 - a
    half = qa.shape[0]
    width = qv.shape[1]
    vrows = qv.shape[0]
    wide = width // 2
    arows = 2 * half
    vblocks = vrows // BLK
    heads = width // HD
    pairs = width // PAIR
    has = {o: (d + o >= 0) & (d + o < n) for o in (-2, -1, 1, 2)}

    def at(vid):
        return {"vid": vid, "aud": a}

    def remote(src, dst, s, r, dev):
        return pltpu.make_async_remote_copy(
            src_ref=src,
            dst_ref=dst,
            send_sem=s,
            recv_sem=r,
            device_id=dev,
            device_id_type=pl.DeviceIdType.MESH,
        )

    def rows(slot, t, size):
        return pl.ds(pl.multiple_of(slot * arows + t * half, half), size)

    barrier = pltpu.get_barrier_semaphore()
    pl.semaphore_signal(
        barrier, inc=1, device_id={"vid": d, "aud": peer}, device_id_type=pl.DeviceIdType.MESH
    )
    for o in has:

        @pl.when(has[o])
        def _(o=o):
            pl.semaphore_signal(
                barrier, inc=1, device_id=at(d + o), device_id_type=pl.DeviceIdType.MESH
            )

    ins = (qa, ga, ka, va)
    own_cols = pl.ds(pl.multiple_of(a * width, PAIR), width)
    peer_cols = pl.ds(pl.multiple_of(peer * width, PAIR), width)
    own_in = [
        pltpu.make_async_copy(
            ins[t].at[:, own_cols], near.at[t, rows(OWN, a, half)], own_sem.at[t]
        )
        for t in range(4)
    ]
    video_in = [
        pltpu.make_async_copy(src, dst, video_sem.at[t])
        for t, (src, dst) in enumerate(
            ((kv_in, kv), (vv_in, vv), (qv_in, qv), (gv_in, gv))
        )
    ]
    video_out = [
        pltpu.make_async_copy(src, dst, write_sem.at[t])
        for t, (src, dst) in enumerate(
            ((out_v, out_v_hbm), (dq_v, dq_v_hbm), (dk_v, dk_v_hbm), (dv_v, dv_v_hbm))
        )
    ]
    for copy in own_in + video_in:
        copy.start()

    pl.semaphore_wait(barrier, 1 + sum(jnp.where(has[o], 1, 0) for o in has))

    x_copy = [
        remote(
            ins[t].at[:, peer_cols],
            near.at[t, rows(OWN, a, half)],
            x_send.at[t],
            x_recv.at[t],
            {"vid": d, "aud": peer},
        )
        for t in range(4)
    ]

    def x_arrived(t):
        return remote(
            ins[t].at[:, own_cols],
            near.at[t, rows(OWN, peer, half)],
            x_send.at[t],
            x_recv.at[t],
            {"vid": d, "aud": peer},
        )

    def piece(group, slot, which):
        return near.at[pl.ds(2 * group, 2), rows(slot, a if which == 0 else peer, half)]

    def far_copy(group, which, side):
        o = (-2, 2)[side]
        return remote(
            piece(group, OWN, which),
            piece(group, OWN - o, which),
            far_send.at[group, which, side],
            far_recv.at[group, which, 1 - side],
            at(d + o),
        )

    def far_arrived(group, which, side):
        o = (-2, 2)[side]
        return remote(
            piece(group, OWN, which),
            piece(group, OWN + o, which),
            far_send.at[group, which, side],
            far_recv.at[group, which, side],
            at(d + o),
        )

    def mate_copy(group, which, slot):
        return remote(
            piece(group, OWN, which),
            piece(group, slot, which),
            mate_send.at[group, which],
            mate_recv.at[group, which],
            at(mate),
        )

    def relay_copy(group, which, src_slot, slot):
        return remote(
            piece(group, src_slot, which),
            piece(group, slot, which),
            relay_send.at[group, which],
            relay_recv.at[group, which],
            at(mate),
        )

    low_slot = 1 + 2 * odd
    high_slot = 3 - 2 * odd
    relay_from = 4 - 4 * odd
    relays_out = ((odd == 0) & has[2]) | ((odd == 1) & has[-2])
    relays_in = ((odd == 0) & has[-1]) | ((odd == 1) & has[1])

    def send_own(group, which):
        for side in range(2):

            @pl.when(has[(-2, 2)[side]])
            def _(side=side):
                far_copy(group, which, side).start()

        mate_copy(group, which, low_slot).start()

    def take_and_relay(group, which):
        for side in range(2):

            @pl.when(has[(-2, 2)[side]])
            def _(side=side):
                far_arrived(group, which, side).wait_recv()

        @pl.when(relays_out)
        def _():
            relay_copy(group, which, relay_from, low_slot + 2 * (1 - 2 * odd)).start()

    def finish_group(group):
        for which in range(2):
            mate_copy(group, which, high_slot).wait_recv()

            @pl.when(relays_in)
            def _(which=which):
                relay_copy(group, which, relay_from, low_slot).wait_recv()

    x_copy[0].start()
    x_copy[1].start()
    for copy in own_in:
        copy.wait()
    send_own(0, 0)
    x_copy[2].start()
    x_copy[3].start()

    for slot in range(SLOTS):
        o = slot - OWN
        if o != 0:

            @pl.when(jnp.logical_not(has[o]))
            def _(slot=slot):
                span = pl.ds(slot * arows, arows)
                near[:, span, :] = jnp.zeros((4, arows, width), BF16)
                stats_in[span, :] = jnp.full((arows, 128), NEG, F32)
                res[span, :] = jnp.zeros((arows, 128), F32)

    for side in range(2):

        @pl.when(jnp.logical_not(has[(-2, 2)[side]]))
        def _(side=side):
            far_in[:, side] = jnp.zeros((2, 2, arows, width), BF16)

    vb = lax.broadcasted_iota(jnp.int32, (arows, vrows), 1) // BLK
    tok = lax.broadcasted_iota(jnp.int32, (arows, vrows), 0)
    tok_l = lax.broadcasted_iota(jnp.int32, (arows, PAIR), 0)
    lens = []
    for slot in range(SLOTS):
        ablk = d + (slot - OWN)
        length = alen[lax.rem(ablk + n, n)]
        lens.append(length)
        bias = jnp.full((arows, vrows), NEG, F32)
        for b in range(vblocks):
            first = win[d * vblocks + b, 0]
            number = win[d * vblocks + b, 1]
            ok = (ablk >= first) & (ablk < first + number)
            bias = jnp.where(vb == b, jnp.where(ok, 0.0, NEG), bias)
        span = pl.ds(slot * arows, arows)
        bias_av[span, :] = bias
        bias_va[span, :] = jnp.where(tok < length, bias, NEG)
        vmask[span, :] = jnp.where(tok_l < length, 1.0, 0.0).astype(BF16)

    lane_w = lax.broadcasted_iota(jnp.int32, (1, PAIR), 1)
    half_mask = [
        jnp.where((lane_w >= HD * h) & (lane_w < HD * (h + 1)), 1.0, 0.0).astype(BF16)
        for h in range(2)
    ]
    lane_s = lax.broadcasted_iota(jnp.int32, (SLOTS * arows, 128), 1)
    stats[...] = jnp.zeros_like(stats)

    def both(low, high):
        lane = lax.broadcasted_iota(jnp.int32, low.shape, 1)
        return jnp.where(lane < HD, low, high)

    x_arrived(0).wait_recv()
    x_arrived(1).wait_recv()
    send_own(0, 1)
    send_own(1, 0)
    take_and_relay(0, 0)
    x_arrived(2).wait_recv()
    x_arrived(3).wait_recv()
    send_own(1, 1)
    take_and_relay(0, 1)
    finish_group(0)

    scale = HD**-0.5

    def cols(i):
        return pl.ds(pl.multiple_of(i * PAIR, PAIR), PAIR)

    def av_scores(i, carry):
        c = cols(i)
        q = near[0, :, c] * jnp.asarray(scale, BF16)
        g = near[1, :, c] * vmask[...]
        k = kv[:, c]
        v = vv[:, c]
        for h in range(2):
            s = dot_nt(q * half_mask[h], k) + bias_av[...]
            dp = dot_nt(g * half_mask[h], v)
            m = jnp.maximum(jnp.max(s, axis=1, keepdims=True), FLOOR)
            e = jnp.exp(s - m)
            total = jnp.sum(e, axis=1, keepdims=True)
            mixed = jnp.sum(e * dp, axis=1, keepdims=True)
            e_buf[2 * i + h] = e
            dp_buf[2 * i + h] = dp
            head = 2 * i + h
            old = stats[...]
            old = jnp.where(lane_s == head, m, old)
            old = jnp.where(lane_s == head + heads, total, old)
            stats[...] = jnp.where(lane_s == head + 2 * heads, mixed, old)
        return carry

    video_in[0].wait()
    video_in[1].wait()
    lax.fori_loop(0, pairs, av_scores, 0)

    def stats_copy(o):
        src = pl.ds((OWN + o) * arows, arows)
        dst = pl.ds((OWN - o) * arows, arows)
        return remote(
            stats.at[src], stats_in.at[dst], st_send.at[OWN + o], st_recv.at[OWN - o], at(d + o)
        )

    def stats_arrived(o):
        span = pl.ds((OWN + o) * arows, arows)
        return remote(
            stats.at[span], stats_in.at[span], st_send.at[OWN + o], st_recv.at[OWN + o], at(d + o)
        )

    def res_copy(o):
        return remote(
            res.at[pl.ds(OWN * arows, arows)],
            res.at[pl.ds((OWN - o) * arows, arows)],
            rs_send.at[OWN + o],
            rs_recv.at[OWN - o],
            at(d + o),
        )

    def res_arrived(o):
        return remote(
            res.at[pl.ds(OWN * arows, arows)],
            res.at[pl.ds((OWN + o) * arows, arows)],
            rs_send.at[OWN + o],
            rs_recv.at[OWN + o],
            at(d + o),
        )

    def each(make, action):
        for o in has:

            @pl.when(has[o])
            def _(o=o):
                action(make(o))

    each(stats_copy, lambda c: c.start())
    own_span = pl.ds(OWN * arows, arows)
    stats_in[own_span, :] = stats[own_span, :]

    take_and_relay(1, 0)
    take_and_relay(1, 1)
    finish_group(1)
    video_in[2].wait()
    video_in[3].wait()

    def store_part(kind, member, c, value):
        part[kind, member, :, c] = value
        sendb[kind, member, :, c] = value.astype(BF16)

    def va_all(i, carry):
        c = cols(i)
        k = near[2, :, c]
        v = near[3, :, c]
        q = qv[:, c] * jnp.asarray(scale, BF16)
        g = gv[:, c]
        o, dq, dk, dv = [], [], [], []
        for h in range(2):
            s = dot_nt(k * half_mask[h], q) + bias_va[...]
            dp = dot_nt(v * half_mask[h], g)
            m = jnp.max(s, axis=0, keepdims=True)
            e = jnp.exp(s - m)
            p = e * (1.0 / jnp.sum(e, axis=0, keepdims=True))
            delta = jnp.sum(p * dp, axis=0, keepdims=True)
            pb = p.astype(BF16)
            ds = (p * (dp - delta)).astype(BF16)
            o.append(dot_tn(pb, v))
            dq.append(dot_tn(ds, k))
            dk.append(dot_nn(ds, q))
            dv.append(dot_nn(pb, g))
        out_v[:, c] = both(*o).astype(BF16)
        dq_v[:, c] = (both(*dq) * scale).astype(BF16)
        store_part(0, 0, c, both(*dk))
        store_part(0, 1, c, both(*dv))
        return carry

    lax.fori_loop(0, pairs // 2, va_all, 0)

    each(stats_arrived, lambda c: c.wait_recv())
    parts = [stats_in[pl.ds(slot * arows, arows), :] for slot in range(SLOTS)]
    top = functools.reduce(jnp.maximum, parts)
    total = jnp.zeros_like(top)
    mixed = jnp.zeros_like(top)
    for x in parts:
        weight = jnp.exp(x - top)
        total = total + weight * pltpu.roll(x, 128 - heads, 1)
        mixed = mixed + weight * pltpu.roll(x, 128 - 2 * heads, 1)
    lane_o = lax.broadcasted_iota(jnp.int32, top.shape, 1)
    res[own_span, :] = jnp.where(
        lane_o < heads, top + jnp.log(total), pltpu.roll(mixed / total, heads, 1)
    )
    each(res_copy, lambda c: c.start())


    def part_of(hf):
        return pl.ds(hf * wide, wide)

    def rm_copy(kind, hf, to_owner, src_slot):
        span = pl.ds(pl.multiple_of(src_slot * arows, arows), arows)
        return remote(
            sendb.at[kind, :, span, part_of(hf)],
            mate_in.at[kind, to_owner, :, :, part_of(hf)],
            rm_send.at[kind, hf, to_owner],
            rm_recv.at[kind, hf, to_owner],
            at(mate),
        )

    def rf_copy(kind, hf, side):
        slot = (0, 4)[side]
        return remote(
            sendb.at[kind, :, pl.ds(slot * arows, arows), part_of(hf)],
            far_in.at[kind, 1 - side, :, :, part_of(hf)],
            rf_send.at[kind, hf, side],
            rf_recv.at[kind, hf, 1 - side],
            at(d + (-2, 2)[side]),
        )

    def rf_arrived(kind, hf, side):
        return remote(
            sendb.at[kind, :, pl.ds(0, arows), part_of(hf)],
            far_in.at[kind, side, :, :, part_of(hf)],
            rf_send.at[kind, hf, side],
            rf_recv.at[kind, hf, side],
            at(d + (-2, 2)[side]),
        )

    def return_first(kind, hf):
        @pl.when(relays_in)
        def _():
            rm_copy(kind, hf, 0, low_slot).start()

        @pl.when((odd == 0) & has[-2])
        def _():
            rf_copy(kind, hf, 0).start()

        @pl.when((odd == 1) & has[2])
        def _():
            rf_copy(kind, hf, 1).start()

        rm_copy(kind, hf, 1, high_slot).start()

    def return_second(kind, hf):
        for side, parity in ((1, 0), (0, 1)):

            @pl.when((odd == parity) & has[(-2, 2)[side]])
            def _(side=side):
                rm_copy(kind, hf, 0, low_slot).wait_recv()
                span = pl.ds((0, 4)[side] * arows, arows)
                for member in range(2):
                    sendb[kind, member, span, part_of(hf)] = (
                        part[kind, member, span, part_of(hf)]
                        + mate_in[kind, 0, member, :, part_of(hf)].astype(F32)
                    ).astype(BF16)
                rf_copy(kind, hf, side).start()

    finals = ((dk_a, dv_a), (out_a, dq_a))

    def span_of(index, hf):
        return pl.ds(pl.multiple_of(index * width + hf * wide, PAIR), wide)

    def xo_copy(kind, hf, member, landing):
        return remote(
            fin.at[kind, member, pl.ds(pl.multiple_of(peer * half, half), half), part_of(hf)],
            finals[kind][member].at[:, span_of(landing, hf)],
            xo_send.at[kind, hf, member],
            xo_recv.at[kind, hf, member],
            {"vid": d, "aud": peer},
        )

    def fin_copy(kind, hf, member):
        return pltpu.make_async_copy(
            fin.at[kind, member, pl.ds(pl.multiple_of(a * half, half), half), part_of(hf)],
            finals[kind][member].at[:, span_of(a, hf)],
            fin_sem.at[kind, hf, member],
        )

    def return_last(kind, hf):
        rm_copy(kind, hf, 1, high_slot).wait_recv()
        for side in range(2):

            @pl.when(has[(-2, 2)[side]])
            def _(side=side):
                rf_arrived(kind, hf, side).wait_recv()

        for member in range(2):
            value = (
                part[kind, member, own_span, part_of(hf)]
                + mate_in[kind, 1, member, :, part_of(hf)].astype(F32)
                + far_in[kind, 0, member, :, part_of(hf)].astype(F32)
                + far_in[kind, 1, member, :, part_of(hf)].astype(F32)
            )
            if kind == 1 and member == 0:
                token = lax.broadcasted_iota(jnp.int32, value.shape, 0)
                value = jnp.where(token < lens[OWN], value, 0.0)
            fin[kind, member, :, part_of(hf)] = value.astype(BF16)
            xo_copy(kind, hf, member, a).start()
            fin_copy(kind, hf, member).start()

    return_first(0, 0)
    lax.fori_loop(pairs // 2, pairs, va_all, 0)
    video_out[0].start()
    video_out[1].start()
    return_first(0, 1)
    return_second(0, 0)
    each(res_arrived, lambda c: c.wait_recv())

    def av_all(i, carry):
        c = cols(i)
        q = near[0, :, c] * jnp.asarray(scale, BF16)
        g = near[1, :, c] * vmask[...]
        k = kv[:, c]
        v = vv[:, c]
        o, dq, dk, dv = [], [], [], []
        lane = lax.broadcasted_iota(jnp.int32, (SLOTS * arows, 128), 1)
        for h in range(2):
            head = 2 * i + h
            gap = jnp.sum(jnp.where(lane == head, stats[...] - res[...], 0.0), 1, keepdims=True)
            delta = jnp.sum(jnp.where(lane == head + heads, res[...], 0.0), 1, keepdims=True)
            p = e_buf[head] * jnp.exp(gap)
            pb = p.astype(BF16)
            ds = (p * (dp_buf[head] - delta)).astype(BF16)
            o.append(dot_nn(pb, v))
            dq.append(dot_nn(ds, k))
            dk.append(dot_tn(ds, q))
            dv.append(dot_tn(pb, g))
        store_part(1, 0, c, both(*o))
        store_part(1, 1, c, both(*dq) * scale)
        dk_v[:, c] = both(*dk).astype(BF16)
        dv_v[:, c] = both(*dv).astype(BF16)
        return carry

    lax.fori_loop(0, pairs // 2, av_all, 0)
    return_first(1, 0)
    return_second(0, 1)
    lax.fori_loop(pairs // 2, pairs, av_all, 0)
    return_first(1, 1)
    video_out[2].start()
    video_out[3].start()
    return_second(1, 0)
    return_second(1, 1)
    order = ((0, 0), (0, 1), (1, 0), (1, 1))
    for kind, hf in order:
        return_last(kind, hf)
    for kind, hf in order:
        for member in range(2):
            xo_copy(kind, hf, member, peer).wait_recv()
            fin_copy(kind, hf, member).wait()
    for copy in video_out:
        copy.wait()

    for t in range(4):
        x_copy[t].wait_send()
    for group in range(2):
        for which in range(2):
            for side in range(2):

                @pl.when(has[(-2, 2)[side]])
                def _(group=group, which=which, side=side):
                    far_copy(group, which, side).wait_send()

            mate_copy(group, which, low_slot).wait_send()

            @pl.when(relays_out)
            def _(group=group, which=which):
                relay_copy(group, which, relay_from, high_slot).wait_send()

    each(stats_copy, lambda c: c.wait_send())
    each(res_copy, lambda c: c.wait_send())
    for kind, hf in order:

        @pl.when(relays_in)
        def _(kind=kind, hf=hf):
            rm_copy(kind, hf, 0, low_slot).wait_send()

        rm_copy(kind, hf, 1, high_slot).wait_send()
        for side in range(2):

            @pl.when(has[(-2, 2)[side]])
            def _(kind=kind, hf=hf, side=side):
                rf_copy(kind, hf, side).wait_send()

        for member in range(2):
            xo_copy(kind, hf, member, a).wait_send()


def write_out(*refs):
    count = (len(refs) - 2) // 3
    sources, results, held = (refs[k * count : (k + 1) * count] for k in range(3))
    into, out = refs[-2:]
    reads = [pltpu.make_async_copy(sources[t], held[t], into.at[t]) for t in range(count)]
    writes = [pltpu.make_async_copy(held[t], results[t], out.at[t]) for t in range(count)]
    for copy in reads:
        copy.start()
    for read, write in zip(reads, writes):
        read.wait()
        write.start()
    for copy in writes:
        copy.wait()


def body(n, q_video, k_video, v_video, g_video, q_audio, k_audio, v_audio, g_audio, window, alen):
    vrows, width = q_video.shape
    half, full = q_audio.shape
    arows = 2 * half
    heads = width // HD
    near_rows = SLOTS * arows
    assert arows == BLK and n % 2 == 0 and 3 * heads <= 128 and width % (2 * PAIR) == 0
    video = jax.ShapeDtypeStruct((vrows, width), BF16)
    audio = jax.ShapeDtypeStruct((half, full), BF16)
    dma = pltpu.SemaphoreType.DMA
    hbm = pl.BlockSpec(memory_space=pltpu.HBM)
    smem = pl.BlockSpec(memory_space=pltpu.SMEM)
    sems = [(4,), (2, 2, 2), (2, 2), (2, 2), (SLOTS,), (SLOTS,)] + [(2, 2, 2)] * 3
    outs = (video, audio, video, video, video, audio, audio, audio)
    found = pl.pallas_call(
        functools.partial(kernel, n),
        out_shape=outs,
        in_specs=[smem] * 2 + [hbm] * 8,
        out_specs=(hbm,) * 8,
        scratch_shapes=[
            pltpu.VMEM((4, near_rows, width), BF16),
            pltpu.VMEM((heads, near_rows, vrows), F32),
            pltpu.VMEM((heads, near_rows, vrows), F32),
            pltpu.VMEM((near_rows, vrows), F32),
            pltpu.VMEM((near_rows, vrows), F32),
            pltpu.VMEM((near_rows, PAIR), BF16),
            pltpu.VMEM((near_rows, 128), F32),
            pltpu.VMEM((near_rows, 128), F32),
            pltpu.VMEM((near_rows, 128), F32),
            pltpu.VMEM((2, 2, near_rows, width), F32),
            pltpu.VMEM((2, 2, near_rows, width), BF16),
            pltpu.VMEM((2, 2, 2, arows, width), BF16),
            pltpu.VMEM((2, 2, 2, arows, width), BF16),
            pltpu.VMEM((2, 2, arows, width), BF16),
        ]
        + [pltpu.VMEM((vrows, width), BF16)] * 8
        + [dma((4,)), dma((4,)), dma((4,)), dma((2, 2, 2))]
        + [dma(shape) for shape in sems for _ in range(2)],
        compiler_params=pltpu.CompilerParams(
            collective_id=0, has_side_effects=True, vmem_limit_bytes=VMEM
        ),
    )(window, alen, q_video, k_video, v_video, g_video, q_audio, k_audio, v_audio, g_audio)
    return pl.pallas_call(
        write_out,
        out_shape=outs,
        in_specs=[hbm] * 8,
        out_specs=(hbm,) * 8,
        scratch_shapes=[pltpu.VMEM(x.shape, BF16) for x in outs] + [dma((8,)), dma((8,))],
        compiler_params=pltpu.CompilerParams(vmem_limit_bytes=VMEM),
    )(*found)


def solution(mesh):
    tokens = P("vid", "aud")
    stretch = P(("vid", "aud"), None)
    return jax.shard_map(
        functools.partial(body, mesh.shape["vid"]),
        mesh=mesh,
        in_specs=(tokens,) * 4 + (stretch,) * 4 + (P(), P()),
        out_specs=(tokens, stretch, tokens, tokens, tokens, stretch, stretch, stretch),
        check_vma=False,
    )
```

```python
import functools

import jax
import jax.numpy as jnp
from jax import lax
from jax.experimental import pallas as pl
from jax.experimental.pallas import tpu as pltpu
from jax.sharding import PartitionSpec as P

HD = 64
BLK = 64
WMAX = 3
NEG = -1e30
FLOOR = -1e29
REACH = WMAX - 1
SLOTS = 2 * REACH + 1
OWN = REACH
PAIR = 2 * HD
VMEM = 62 * 1024 * 1024

F32 = jnp.float32
BF16 = jnp.bfloat16


def dot_nt(a, b):
    return lax.dot_general(a, b, (((1,), (1,)), ((), ())), preferred_element_type=F32)


def dot_nn(a, b):
    return lax.dot_general(a, b, (((1,), (0,)), ((), ())), preferred_element_type=F32)


def dot_tn(a, b):
    return lax.dot_general(a, b, (((0,), (0,)), ((), ())), preferred_element_type=F32)


def kernel(
    n,
    win,
    alen,
    qv_in,
    kv_in,
    vv_in,
    gv_in,
    qa,
    ka,
    va,
    ga,
    out_v_hbm,
    out_a,
    dq_v_hbm,
    dk_v_hbm,
    dv_v_hbm,
    dq_a,
    dk_a,
    dv_a,
    near,
    e_buf,
    dp_buf,
    bias_va,
    bias_av,
    vmask,
    stats,
    stats_in,
    res,
    part,
    sendb,
    mate_in,
    far_in,
    fin,
    qv,
    kv,
    vv,
    gv,
    out_v,
    dq_v,
    dk_v,
    dv_v,
    own_sem,
    video_sem,
    write_sem,
    fin_sem,
    x_send,
    x_recv,
    far_send,
    far_recv,
    mate_send,
    mate_recv,
    relay_send,
    relay_recv,
    st_send,
    st_recv,
    rs_send,
    rs_recv,
    rm_send,
    rm_recv,
    rf_send,
    rf_recv,
    xo_send,
    xo_recv,
):
    d = lax.axis_index("vid")
    a = lax.axis_index("aud")
    odd = lax.rem(d, 2)
    mate = d + 1 - 2 * odd
    peer = 1 - a
    half = qa.shape[0]
    width = qv.shape[1]
    vrows = qv.shape[0]
    wide = width // 2
    arows = 2 * half
    vblocks = vrows // BLK
    heads = width // HD
    pairs = width // PAIR
    has = {o: (d + o >= 0) & (d + o < n) for o in (-2, -1, 1, 2)}

    def at(vid):
        return {"vid": vid, "aud": a}

    def remote(src, dst, s, r, dev):
        return pltpu.make_async_remote_copy(
            src_ref=src,
            dst_ref=dst,
            send_sem=s,
            recv_sem=r,
            device_id=dev,
            device_id_type=pl.DeviceIdType.MESH,
        )

    def rows(slot, t, size):
        return pl.ds(pl.multiple_of(slot * arows + t * half, half), size)

    barrier = pltpu.get_barrier_semaphore()
    pl.semaphore_signal(
        barrier, inc=1, device_id={"vid": d, "aud": peer}, device_id_type=pl.DeviceIdType.MESH
    )
    for o in has:

        @pl.when(has[o])
        def _(o=o):
            pl.semaphore_signal(
                barrier, inc=1, device_id=at(d + o), device_id_type=pl.DeviceIdType.MESH
            )

    ins = (qa, ga, ka, va)
    own_cols = pl.ds(pl.multiple_of(a * width, PAIR), width)
    peer_cols = pl.ds(pl.multiple_of(peer * width, PAIR), width)
    own_in = [
        pltpu.make_async_copy(
            ins[t].at[:, own_cols], near.at[t, rows(OWN, a, half)], own_sem.at[t]
        )
        for t in range(4)
    ]
    video_in = [
        pltpu.make_async_copy(src, dst, video_sem.at[t])
        for t, (src, dst) in enumerate(
            ((kv_in, kv), (vv_in, vv), (qv_in, qv), (gv_in, gv))
        )
    ]
    video_out = [
        pltpu.make_async_copy(src, dst, write_sem.at[t])
        for t, (src, dst) in enumerate(
            ((out_v, out_v_hbm), (dq_v, dq_v_hbm), (dk_v, dk_v_hbm), (dv_v, dv_v_hbm))
        )
    ]
    for copy in own_in:
        copy.start()

    pl.semaphore_wait(barrier, 1 + sum(jnp.where(has[o], 1, 0) for o in has))

    x_copy = [
        remote(
            ins[t].at[:, peer_cols],
            near.at[t, rows(OWN, a, half)],
            x_send.at[t],
            x_recv.at[t],
            {"vid": d, "aud": peer},
        )
        for t in range(4)
    ]

    def x_arrived(t):
        return remote(
            ins[t].at[:, own_cols],
            near.at[t, rows(OWN, peer, half)],
            x_send.at[t],
            x_recv.at[t],
            {"vid": d, "aud": peer},
        )

    def piece(group, slot, which):
        return near.at[pl.ds(2 * group, 2), rows(slot, a if which == 0 else peer, half)]

    def far_copy(group, which, side):
        o = (-2, 2)[side]
        return remote(
            piece(group, OWN, which),
            piece(group, OWN - o, which),
            far_send.at[group, which, side],
            far_recv.at[group, which, 1 - side],
            at(d + o),
        )

    def far_arrived(group, which, side):
        o = (-2, 2)[side]
        return remote(
            piece(group, OWN, which),
            piece(group, OWN + o, which),
            far_send.at[group, which, side],
            far_recv.at[group, which, side],
            at(d + o),
        )

    def mate_copy(group, which, slot):
        return remote(
            piece(group, OWN, which),
            piece(group, slot, which),
            mate_send.at[group, which],
            mate_recv.at[group, which],
            at(mate),
        )

    def relay_copy(group, which, src_slot, slot):
        return remote(
            piece(group, src_slot, which),
            piece(group, slot, which),
            relay_send.at[group, which],
            relay_recv.at[group, which],
            at(mate),
        )

    low_slot = 1 + 2 * odd
    high_slot = 3 - 2 * odd
    relay_from = 4 - 4 * odd
    relays_out = ((odd == 0) & has[2]) | ((odd == 1) & has[-2])
    relays_in = ((odd == 0) & has[-1]) | ((odd == 1) & has[1])

    def send_own(group, which):
        for side in range(2):

            @pl.when(has[(-2, 2)[side]])
            def _(side=side):
                far_copy(group, which, side).start()

        mate_copy(group, which, low_slot).start()

    def take_and_relay(group, which):
        for side in range(2):

            @pl.when(has[(-2, 2)[side]])
            def _(side=side):
                far_arrived(group, which, side).wait_recv()

        @pl.when(relays_out)
        def _():
            relay_copy(group, which, relay_from, low_slot + 2 * (1 - 2 * odd)).start()

    def finish_group(group):
        for which in range(2):
            mate_copy(group, which, high_slot).wait_recv()

            @pl.when(relays_in)
            def _(which=which):
                relay_copy(group, which, relay_from, low_slot).wait_recv()

    x_copy[0].start()
    x_copy[1].start()
    own_in[0].wait()
    own_in[1].wait()
    send_own(0, 0)
    x_copy[2].start()
    x_copy[3].start()
    own_in[2].wait()
    own_in[3].wait()
    send_own(1, 0)
    for copy in video_in:
        copy.start()

    for slot in range(SLOTS):
        o = slot - OWN
        if o != 0:

            @pl.when(jnp.logical_not(has[o]))
            def _(slot=slot):
                span = pl.ds(slot * arows, arows)
                near[:, span, :] = jnp.zeros((4, arows, width), BF16)
                stats_in[span, :] = jnp.full((arows, 128), NEG, F32)
                res[span, :] = jnp.zeros((arows, 128), F32)

    for side in range(2):

        @pl.when(jnp.logical_not(has[(-2, 2)[side]]))
        def _(side=side):
            far_in[:, side] = jnp.zeros((2, 2, arows, width), BF16)

    vb = lax.broadcasted_iota(jnp.int32, (arows, vrows), 1) // BLK
    tok = lax.broadcasted_iota(jnp.int32, (arows, vrows), 0)
    tok_l = lax.broadcasted_iota(jnp.int32, (arows, PAIR), 0)
    lens = []
    for slot in range(SLOTS):
        ablk = d + (slot - OWN)
        length = alen[lax.rem(ablk + n, n)]
        lens.append(length)
        bias = jnp.full((arows, vrows), NEG, F32)
        for b in range(vblocks):
            first = win[d * vblocks + b, 0]
            number = win[d * vblocks + b, 1]
            ok = (ablk >= first) & (ablk < first + number)
            bias = jnp.where(vb == b, jnp.where(ok, 0.0, NEG), bias)
        span = pl.ds(slot * arows, arows)
        bias_av[span, :] = bias
        bias_va[span, :] = jnp.where(tok < length, bias, NEG)
        vmask[span, :] = jnp.where(tok_l < length, 1.0, 0.0).astype(BF16)

    lane_w = lax.broadcasted_iota(jnp.int32, (1, PAIR), 1)
    half_mask = [
        jnp.where((lane_w >= HD * h) & (lane_w < HD * (h + 1)), 1.0, 0.0).astype(BF16)
        for h in range(2)
    ]
    lane_s = lax.broadcasted_iota(jnp.int32, (SLOTS * arows, 128), 1)
    stats[...] = jnp.zeros_like(stats)

    def both(low, high):
        lane = lax.broadcasted_iota(jnp.int32, low.shape, 1)
        return jnp.where(lane < HD, low, high)

    x_arrived(0).wait_recv()
    x_arrived(1).wait_recv()
    send_own(0, 1)
    take_and_relay(0, 0)
    x_arrived(2).wait_recv()
    x_arrived(3).wait_recv()
    send_own(1, 1)
    take_and_relay(0, 1)
    finish_group(0)

    scale = HD**-0.5

    def cols(i):
        return pl.ds(pl.multiple_of(i * PAIR, PAIR), PAIR)

    def av_scores(i, carry):
        c = cols(i)
        q = near[0, :, c] * jnp.asarray(scale, BF16)
        g = near[1, :, c] * vmask[...]
        k = kv[:, c]
        v = vv[:, c]
        for h in range(2):
            s = dot_nt(q * half_mask[h], k) + bias_av[...]
            dp = dot_nt(g * half_mask[h], v)
            m = jnp.maximum(jnp.max(s, axis=1, keepdims=True), FLOOR)
            e = jnp.exp(s - m)
            total = jnp.sum(e, axis=1, keepdims=True)
            mixed = jnp.sum(e * dp, axis=1, keepdims=True)
            e_buf[2 * i + h] = e
            dp_buf[2 * i + h] = dp
            head = 2 * i + h
            old = stats[...]
            old = jnp.where(lane_s == head, m, old)
            old = jnp.where(lane_s == head + heads, total, old)
            stats[...] = jnp.where(lane_s == head + 2 * heads, mixed, old)
        return carry

    video_in[0].wait()
    video_in[1].wait()
    lax.fori_loop(0, pairs, av_scores, 0)

    def stats_copy(o):
        src = pl.ds((OWN + o) * arows, arows)
        dst = pl.ds((OWN - o) * arows, arows)
        return remote(
            stats.at[src], stats_in.at[dst], st_send.at[OWN + o], st_recv.at[OWN - o], at(d + o)
        )

    def stats_arrived(o):
        span = pl.ds((OWN + o) * arows, arows)
        return remote(
            stats.at[span], stats_in.at[span], st_send.at[OWN + o], st_recv.at[OWN + o], at(d + o)
        )

    def res_copy(o):
        return remote(
            res.at[pl.ds(OWN * arows, arows)],
            res.at[pl.ds((OWN - o) * arows, arows)],
            rs_send.at[OWN + o],
            rs_recv.at[OWN - o],
            at(d + o),
        )

    def res_arrived(o):
        return remote(
            res.at[pl.ds(OWN * arows, arows)],
            res.at[pl.ds((OWN + o) * arows, arows)],
            rs_send.at[OWN + o],
            rs_recv.at[OWN + o],
            at(d + o),
        )

    def each(make, action):
        for o in has:

            @pl.when(has[o])
            def _(o=o):
                action(make(o))

    each(stats_copy, lambda c: c.start())
    own_span = pl.ds(OWN * arows, arows)
    stats_in[own_span, :] = stats[own_span, :]

    take_and_relay(1, 0)
    take_and_relay(1, 1)
    finish_group(1)
    video_in[2].wait()
    video_in[3].wait()

    def store_part(kind, member, c, value):
        part[kind, member, :, c] = value
        sendb[kind, member, :, c] = value.astype(BF16)

    def va_all(i, carry):
        c = cols(i)
        k = near[2, :, c]
        v = near[3, :, c]
        q = qv[:, c] * jnp.asarray(scale, BF16)
        g = gv[:, c]
        o, dq, dk, dv = [], [], [], []
        for h in range(2):
            s = dot_nt(k * half_mask[h], q) + bias_va[...]
            dp = dot_nt(v * half_mask[h], g)
            m = jnp.max(s, axis=0, keepdims=True)
            e = jnp.exp(s - m)
            p = e * (1.0 / jnp.sum(e, axis=0, keepdims=True))
            delta = jnp.sum(p * dp, axis=0, keepdims=True)
            pb = p.astype(BF16)
            ds = (p * (dp - delta)).astype(BF16)
            o.append(dot_tn(pb, v))
            dq.append(dot_tn(ds, k))
            dk.append(dot_nn(ds, q))
            dv.append(dot_nn(pb, g))
        out_v[:, c] = both(*o).astype(BF16)
        dq_v[:, c] = (both(*dq) * scale).astype(BF16)
        store_part(0, 0, c, both(*dk))
        store_part(0, 1, c, both(*dv))
        return carry

    lax.fori_loop(0, pairs // 2, va_all, 0)

    each(stats_arrived, lambda c: c.wait_recv())
    parts = [stats_in[pl.ds(slot * arows, arows), :] for slot in range(SLOTS)]
    top = functools.reduce(jnp.maximum, parts)
    total = jnp.zeros_like(top)
    mixed = jnp.zeros_like(top)
    for x in parts:
        weight = jnp.exp(x - top)
        total = total + weight * pltpu.roll(x, 128 - heads, 1)
        mixed = mixed + weight * pltpu.roll(x, 128 - 2 * heads, 1)
    lane_o = lax.broadcasted_iota(jnp.int32, top.shape, 1)
    res[own_span, :] = jnp.where(
        lane_o < heads, top + jnp.log(total), pltpu.roll(mixed / total, heads, 1)
    )
    each(res_copy, lambda c: c.start())


    def part_of(hf):
        return pl.ds(hf * wide, wide)

    def rm_copy(kind, hf, to_owner, src_slot):
        span = pl.ds(pl.multiple_of(src_slot * arows, arows), arows)
        return remote(
            sendb.at[kind, :, span, part_of(hf)],
            mate_in.at[kind, to_owner, :, :, part_of(hf)],
            rm_send.at[kind, hf, to_owner],
            rm_recv.at[kind, hf, to_owner],
            at(mate),
        )

    def rf_copy(kind, hf, side):
        slot = (0, 4)[side]
        return remote(
            sendb.at[kind, :, pl.ds(slot * arows, arows), part_of(hf)],
            far_in.at[kind, 1 - side, :, :, part_of(hf)],
            rf_send.at[kind, hf, side],
            rf_recv.at[kind, hf, 1 - side],
            at(d + (-2, 2)[side]),
        )

    def rf_arrived(kind, hf, side):
        return remote(
            sendb.at[kind, :, pl.ds(0, arows), part_of(hf)],
            far_in.at[kind, side, :, :, part_of(hf)],
            rf_send.at[kind, hf, side],
            rf_recv.at[kind, hf, side],
            at(d + (-2, 2)[side]),
        )

    def return_first(kind, hf):
        @pl.when(relays_in)
        def _():
            rm_copy(kind, hf, 0, low_slot).start()

        @pl.when((odd == 0) & has[-2])
        def _():
            rf_copy(kind, hf, 0).start()

        @pl.when((odd == 1) & has[2])
        def _():
            rf_copy(kind, hf, 1).start()

        rm_copy(kind, hf, 1, high_slot).start()

    def return_second(kind, hf):
        for side, parity in ((1, 0), (0, 1)):

            @pl.when((odd == parity) & has[(-2, 2)[side]])
            def _(side=side):
                rm_copy(kind, hf, 0, low_slot).wait_recv()
                span = pl.ds((0, 4)[side] * arows, arows)
                for member in range(2):
                    sendb[kind, member, span, part_of(hf)] = (
                        part[kind, member, span, part_of(hf)]
                        + mate_in[kind, 0, member, :, part_of(hf)].astype(F32)
                    ).astype(BF16)
                rf_copy(kind, hf, side).start()

    finals = ((dk_a, dv_a), (out_a, dq_a))

    def span_of(index, hf):
        return pl.ds(pl.multiple_of(index * width + hf * wide, PAIR), wide)

    def xo_copy(kind, hf, member, landing):
        return remote(
            fin.at[kind, member, pl.ds(pl.multiple_of(peer * half, half), half), part_of(hf)],
            finals[kind][member].at[:, span_of(landing, hf)],
            xo_send.at[kind, hf, member],
            xo_recv.at[kind, hf, member],
            {"vid": d, "aud": peer},
        )

    def fin_copy(kind, hf, member):
        return pltpu.make_async_copy(
            fin.at[kind, member, pl.ds(pl.multiple_of(a * half, half), half), part_of(hf)],
            finals[kind][member].at[:, span_of(a, hf)],
            fin_sem.at[kind, hf, member],
        )

    def return_last(kind, hf):
        rm_copy(kind, hf, 1, high_slot).wait_recv()
        for side in range(2):

            @pl.when(has[(-2, 2)[side]])
            def _(side=side):
                rf_arrived(kind, hf, side).wait_recv()

        for member in range(2):
            value = (
                part[kind, member, own_span, part_of(hf)]
                + mate_in[kind, 1, member, :, part_of(hf)].astype(F32)
                + far_in[kind, 0, member, :, part_of(hf)].astype(F32)
                + far_in[kind, 1, member, :, part_of(hf)].astype(F32)
            )
            if kind == 1 and member == 0:
                token = lax.broadcasted_iota(jnp.int32, value.shape, 0)
                value = jnp.where(token < lens[OWN], value, 0.0)
            fin[kind, member, :, part_of(hf)] = value.astype(BF16)
            xo_copy(kind, hf, member, a).start()
            fin_copy(kind, hf, member).start()

    return_first(0, 0)
    lax.fori_loop(pairs // 2, pairs, va_all, 0)
    video_out[0].start()
    video_out[1].start()
    return_first(0, 1)
    return_second(0, 0)
    each(res_arrived, lambda c: c.wait_recv())

    def av_all(i, carry):
        c = cols(i)
        q = near[0, :, c] * jnp.asarray(scale, BF16)
        g = near[1, :, c] * vmask[...]
        k = kv[:, c]
        v = vv[:, c]
        o, dq, dk, dv = [], [], [], []
        lane = lax.broadcasted_iota(jnp.int32, (SLOTS * arows, 128), 1)
        for h in range(2):
            head = 2 * i + h
            gap = jnp.sum(jnp.where(lane == head, stats[...] - res[...], 0.0), 1, keepdims=True)
            delta = jnp.sum(jnp.where(lane == head + heads, res[...], 0.0), 1, keepdims=True)
            p = e_buf[head] * jnp.exp(gap)
            pb = p.astype(BF16)
            ds = (p * (dp_buf[head] - delta)).astype(BF16)
            o.append(dot_nn(pb, v))
            dq.append(dot_nn(ds, k))
            dk.append(dot_tn(ds, q))
            dv.append(dot_tn(pb, g))
        store_part(1, 0, c, both(*o))
        store_part(1, 1, c, both(*dq) * scale)
        dk_v[:, c] = both(*dk).astype(BF16)
        dv_v[:, c] = both(*dv).astype(BF16)
        return carry

    lax.fori_loop(0, pairs // 2, av_all, 0)
    return_first(1, 0)
    return_second(0, 1)
    lax.fori_loop(pairs // 2, pairs, av_all, 0)
    return_first(1, 1)
    video_out[2].start()
    video_out[3].start()
    return_second(1, 0)
    return_second(1, 1)
    order = ((0, 0), (0, 1), (1, 0), (1, 1))
    for kind, hf in order:
        return_last(kind, hf)
    for kind, hf in order:
        for member in range(2):
            xo_copy(kind, hf, member, peer).wait_recv()
            fin_copy(kind, hf, member).wait()
    for copy in video_out:
        copy.wait()

    for t in range(4):
        x_copy[t].wait_send()
    for group in range(2):
        for which in range(2):
            for side in range(2):

                @pl.when(has[(-2, 2)[side]])
                def _(group=group, which=which, side=side):
                    far_copy(group, which, side).wait_send()

            mate_copy(group, which, low_slot).wait_send()

            @pl.when(relays_out)
            def _(group=group, which=which):
                relay_copy(group, which, relay_from, high_slot).wait_send()

    each(stats_copy, lambda c: c.wait_send())
    each(res_copy, lambda c: c.wait_send())
    for kind, hf in order:

        @pl.when(relays_in)
        def _(kind=kind, hf=hf):
            rm_copy(kind, hf, 0, low_slot).wait_send()

        rm_copy(kind, hf, 1, high_slot).wait_send()
        for side in range(2):

            @pl.when(has[(-2, 2)[side]])
            def _(kind=kind, hf=hf, side=side):
                rf_copy(kind, hf, side).wait_send()

        for member in range(2):
            xo_copy(kind, hf, member, a).wait_send()


def write_out(*refs):
    count = (len(refs) - 2) // 3
    sources, results, held = (refs[k * count : (k + 1) * count] for k in range(3))
    into, out = refs[-2:]
    reads = [pltpu.make_async_copy(sources[t], held[t], into.at[t]) for t in range(count)]
    writes = [pltpu.make_async_copy(held[t], results[t], out.at[t]) for t in range(count)]
    for copy in reads:
        copy.start()
    for read, write in zip(reads, writes):
        read.wait()
        write.start()
    for copy in writes:
        copy.wait()


def body(n, q_video, k_video, v_video, g_video, q_audio, k_audio, v_audio, g_audio, window, alen):
    vrows, width = q_video.shape
    half, full = q_audio.shape
    arows = 2 * half
    heads = width // HD
    near_rows = SLOTS * arows
    assert arows == BLK and n % 2 == 0 and 3 * heads <= 128 and width % (2 * PAIR) == 0
    video = jax.ShapeDtypeStruct((vrows, width), BF16)
    audio = jax.ShapeDtypeStruct((half, full), BF16)
    dma = pltpu.SemaphoreType.DMA
    hbm = pl.BlockSpec(memory_space=pltpu.HBM)
    smem = pl.BlockSpec(memory_space=pltpu.SMEM)
    sems = [(4,), (2, 2, 2), (2, 2), (2, 2), (SLOTS,), (SLOTS,)] + [(2, 2, 2)] * 3
    outs = (video, audio, video, video, video, audio, audio, audio)
    found = pl.pallas_call(
        functools.partial(kernel, n),
        out_shape=outs,
        in_specs=[smem] * 2 + [hbm] * 8,
        out_specs=(hbm,) * 8,
        scratch_shapes=[
            pltpu.VMEM((4, near_rows, width), BF16),
            pltpu.VMEM((heads, near_rows, vrows), F32),
            pltpu.VMEM((heads, near_rows, vrows), F32),
            pltpu.VMEM((near_rows, vrows), F32),
            pltpu.VMEM((near_rows, vrows), F32),
            pltpu.VMEM((near_rows, PAIR), BF16),
            pltpu.VMEM((near_rows, 128), F32),
            pltpu.VMEM((near_rows, 128), F32),
            pltpu.VMEM((near_rows, 128), F32),
            pltpu.VMEM((2, 2, near_rows, width), F32),
            pltpu.VMEM((2, 2, near_rows, width), BF16),
            pltpu.VMEM((2, 2, 2, arows, width), BF16),
            pltpu.VMEM((2, 2, 2, arows, width), BF16),
            pltpu.VMEM((2, 2, arows, width), BF16),
        ]
        + [pltpu.VMEM((vrows, width), BF16)] * 8
        + [dma((4,)), dma((4,)), dma((4,)), dma((2, 2, 2))]
        + [dma(shape) for shape in sems for _ in range(2)],
        compiler_params=pltpu.CompilerParams(
            collective_id=0, has_side_effects=True, vmem_limit_bytes=VMEM
        ),
    )(window, alen, q_video, k_video, v_video, g_video, q_audio, k_audio, v_audio, g_audio)
    return pl.pallas_call(
        write_out,
        out_shape=outs,
        in_specs=[hbm] * 8,
        out_specs=(hbm,) * 8,
        scratch_shapes=[pltpu.VMEM(x.shape, BF16) for x in outs] + [dma((8,)), dma((8,))],
        compiler_params=pltpu.CompilerParams(vmem_limit_bytes=VMEM),
    )(*found)


def solution(mesh):
    tokens = P("vid", "aud")
    stretch = P(("vid", "aud"), None)
    return jax.shard_map(
        functools.partial(body, mesh.shape["vid"]),
        mesh=mesh,
        in_specs=(tokens,) * 4 + (stretch,) * 4 + (P(), P()),
        out_specs=(tokens, stretch, tokens, tokens, tokens, stretch, stretch, stretch),
        check_vma=False,
    )
```
